512 devices in a mesh: group: 16 (over x, y_hi, core), blk: 32 (over y_lo, z).
Axes of the slice: x: 4, y: 4 (y_hi: 2, y_lo: 2; y = y_hi * 2 + y_lo), z: 16, core: 2. Of those that a mesh axis runs over, the one named last changes fastest.
Arguments:
- tokens: bfloat16 [16384, 2048], P(('group', 'blk')), may hold values from -6 to 6
- expert_ids: int32 [16384, 4], P(('group', 'blk')), may hold values from 0 to 127, all different within a row; in each aligned block of 32 rows (0 to 31, 32 to 63, ...) at most 2 rows name the same one
- grad_hidden: bfloat16 [16384, 4, 768], P(('group', 'blk')), may hold values from -6 to 6
- gate_blocks: bfloat16 [512, 192, 2048], P(('group', 'blk')), may hold values from -0.125 to 0.125
- up_blocks: bfloat16 [512, 192, 2048], P(('group', 'blk')), may hold values from -0.125 to 0.125
Outputs:
- hidden_out: bfloat16 [16384, 4, 768], P(('group', 'blk'))
- grad_tokens: bfloat16 [16384, 2048], P(('group', 'blk'))
- grad_gate: bfloat16 [512, 192, 2048], P(('group', 'blk'))
- grad_up: bfloat16 [512, 192, 2048], P(('group', 'blk'))
The draws below stay inside these ranges and needn't reach their ends.
Inputs may be any that keep to these rules, and one draw needn't show every extreme that they name: `expert_ids`: each row names 4 different experts. Among the rows of one device no expert is named by more than 2 rows, and in every draw some expert is named by exactly 2 rows of some device.
All inputs are finite; a program needn't handle non-finite values.
Results may differ from the reference program's by a relative error of at most 0.0058.
Values may be sent and summed in bfloat16 or wider, within the bound.
No kernel may reach another device: no remote copies, remote signals or barrier semaphores. Data moves between devices by JAX's collectives and lax.ppermute only.
A program may use at most 64 MiB of HBM per device.

```python
import math
import jax
import jax.numpy as jnp
import numpy as np
from jax import lax

D = 2048
FF = 768
TOPK = 4
TOK_DEV = 32
EXPERTS = 128
FF_BLK = 192
BLOCKS = 512
TOKENS = 16384
CAP = 2
N_GROUP = 16
N_BLK = 32


def shard_levels(rng, extent, shards, least, high):
    loudness = 1.0
    for position, parts in shards:
        draws = jax.random.uniform(jax.random.fold_in(jax.random.fold_in(rng, 6), position), (parts,), jnp.float32, least / len(shards), high / len(shards))
        loudness = loudness * jnp.repeat(jnp.exp(draws), extent[position] // parts).reshape((-1,) + (1,) * (len(extent) - 1 - position))
    return loudness


def deal_out(own_key, own, number, rows, number_of, top, bound, slope):
    sequence = jax.random.permutation(own_key, number_of)
    crowded, ordinary = shares(number_of, rows * top, bound, slope, True), shares(number_of, rows * top, bound, slope, False)
    places = jnp.arange(number_of)

    def named(tallies, offset_by):
        used = int((tallies > 0).sum())
        fixed = max(1, used // 4)
        shifted = fixed + (places - fixed + offset_by * (used - fixed)) % max(1, number_of - fixed)
        return jnp.zeros((number_of,), jnp.int32).at[sequence[jnp.where(places < fixed, places, shifted)]].set(jnp.asarray(tallies, jnp.int32))

    tallies = jnp.where(number % 4 == 0, named(crowded, number // 4), named(ordinary, number - number // 4 - 1))
    mixed = jax.random.permutation(jax.random.fold_in(own, 3), number_of)
    giver, sink = mixed[0:number_of // 2 * 2:2], mixed[1:number_of // 2 * 2:2]
    margin = jnp.minimum(tallies[giver] - 1, bound - tallies[sink]) // 2
    margin = jnp.where((giver == sequence[0]) | (sink == sequence[0]) | (tallies[sink] == 0), 0, jnp.maximum(margin, 0))
    shifted = jax.random.randint(jax.random.fold_in(own, 4), (number_of // 2,), 0, 1 << 20) % (margin + 1)
    tallies = tallies.at[giver].add(-shifted).at[sink].add(shifted)
    members = jnp.searchsorted(jnp.cumsum(tallies), jnp.arange(rows * top), side="right").astype(jnp.int32)
    table = members.reshape(top, rows).T
    table = table[jax.random.permutation(jax.random.fold_in(own, 1), rows)]
    offset_by = jax.random.randint(jax.random.fold_in(own, 2), (rows, 1), 0, top)
    return jnp.take_along_axis(table, (jnp.arange(top)[None, :] + offset_by) % top, axis=1)


def shares(count, total, limit, skew, full):
    portions = [(1 << 20) // math.isqrt(standing ** skew) + 1 for standing in range(1, count + 1)]
    largest = limit if full else min(limit, max(-(-total // count), total * portions[0] // sum(portions)))
    least = 1 if total - largest >= count - 1 else 0
    given, surplus = [largest] + [least] * (count - 1), total - largest - least * (count - 1)
    while surplus > 0:
        movable = [i for i in range(1, count) if given[i] < largest] or [i for i in range(1, count) if given[i] < limit]
        whole, left = sum([portions[i] for i in movable]), surplus
        for i in movable:
            addition = min(limit - given[i], max(1, left * portions[i] // whole), surplus)
            given[i] = given[i] + addition
            surplus = surplus - addition
    return np.array(given)


def gaussian(own_key, dims, deviation, limit, shards=(), kind=jnp.bfloat16):
    drawn = deviation * jax.random.normal(own_key, dims, jnp.float32)
    if shards:
        drawn = drawn * shard_levels(own_key, dims, shards, -0.22, 0.18)
    return jnp.clip(drawn, -limit, limit).astype(kind)


def setup_inputs(seed: int = 0) -> dict:
    streams_of = jax.random.split(jax.random.key(seed), 6)
    tokens = gaussian(streams_of[0], (TOKENS, D), 1.0, 6.0, ((0, 512),))
    expert_ids_keys = jax.random.split(jax.random.fold_in(streams_of[1], 1), TOKENS // TOK_DEV)
    expert_ids_turns = jax.random.permutation(jax.random.fold_in(streams_of[1], 3), TOKENS // TOK_DEV)
    expert_ids = jax.vmap(lambda own, number: deal_out(jax.random.fold_in(streams_of[1], 2), own, number, TOK_DEV, EXPERTS, TOPK, CAP, 2))(expert_ids_keys, expert_ids_turns).reshape((TOKENS, TOPK))
    grad_hidden = gaussian(streams_of[2], (TOKENS, TOPK, FF), 1.0, 6.0, ((0, 512),))
    gate_blocks = gaussian(streams_of[3], (BLOCKS, FF_BLK, D), D ** -0.5, 0.125, ((0, 512),))
    up_blocks = gaussian(streams_of[4], (BLOCKS, FF_BLK, D), D ** -0.5, 0.125, ((0, 512),))
    return {"tokens": tokens, "expert_ids": expert_ids, "grad_hidden": grad_hidden, "gate_blocks": gate_blocks, "up_blocks": up_blocks}


def expert_rows(x_rows, dh_rows, w_gate, w_up):
    gate_pre = lax.dot_general(x_rows, w_gate, (((1,), (1,)), ((), ())), preferred_element_type=jnp.float32)
    up_pre = lax.dot_general(x_rows, w_up, (((1,), (1,)), ((), ())), preferred_element_type=jnp.float32)
    sigmoid_gate = jax.nn.sigmoid(gate_pre)
    active = gate_pre * sigmoid_gate
    hidden = (active * up_pre).astype(jnp.bfloat16)
    upstream = dh_rows.astype(jnp.float32)
    d_gate = (upstream * up_pre * sigmoid_gate * (1.0 + gate_pre * (1.0 - sigmoid_gate))).astype(jnp.bfloat16)
    d_up = (upstream * active).astype(jnp.bfloat16)
    token_term = jnp.dot(d_gate, w_gate, preferred_element_type=jnp.float32) + jnp.dot(d_up, w_up, preferred_element_type=jnp.float32)
    grad_g = lax.dot_general(d_gate, x_rows, (((0,), (0,)), ((), ())), preferred_element_type=jnp.float32)
    grad_u = lax.dot_general(d_up, x_rows, (((0,), (0,)), ((), ())), preferred_element_type=jnp.float32)
    return hidden, token_term.astype(jnp.bfloat16), grad_g.astype(jnp.bfloat16), grad_u.astype(jnp.bfloat16)


def to_full(blocks_in):
    return blocks_in.reshape(EXPERTS, FF, D)


def to_layout(full_in):
    return full_in.reshape(BLOCKS, FF_BLK, D)


def reference(tokens, expert_ids, grad_hidden, gate_blocks, up_blocks):
    w_gate_all = to_full(gate_blocks)
    w_up_all = to_full(up_blocks)
    pair_count = TOKENS * TOPK
    most_rows = N_GROUP * N_BLK * CAP
    flat_ids = expert_ids.reshape(pair_count).astype(jnp.int32)
    sorted_pairs = jnp.argsort(flat_ids, stable=True).astype(jnp.int32)
    counts = jnp.zeros((EXPERTS,), jnp.int32).at[flat_ids].add(1)
    starts = (jnp.cumsum(counts) - counts).astype(jnp.int32)
    padded = jnp.concatenate([sorted_pairs, jnp.zeros((most_rows,), jnp.int32)])
    upstream = grad_hidden.reshape(pair_count, FF)

    def one_expert(state_pair, expert):
        hidden_all, grad_all = state_pair
        row_index = lax.dynamic_slice(padded, (starts[expert],), (most_rows,))
        valid_rows = jnp.arange(most_rows, dtype=jnp.int32) < counts[expert]
        token_index = (row_index // TOPK).astype(jnp.int32)
        x_rows = jnp.where(valid_rows[:, None], tokens[token_index], jnp.zeros((), tokens.dtype))
        dh_rows = jnp.where(valid_rows[:, None], upstream[row_index], jnp.zeros((), upstream.dtype))
        hidden, token_term, grad_g, grad_u = expert_rows(x_rows, dh_rows, w_gate_all[expert], w_up_all[expert])
        target = jnp.where(valid_rows, row_index, pair_count)
        hidden_all = hidden_all.at[target].set(hidden, mode="drop")
        token_target = jnp.where(valid_rows, token_index, TOKENS)
        grad_all = grad_all.at[token_target].add(token_term.astype(grad_all.dtype), mode="drop")
        return (hidden_all, grad_all), (grad_g, grad_u)

    start_state = (jnp.zeros((pair_count, FF), jnp.bfloat16), jnp.zeros((TOKENS, D), jnp.float32))
    final_state, grads = lax.scan(one_expert, start_state, jnp.arange(EXPERTS, dtype=jnp.int32))
    hidden_all, grad_all = final_state
    grad_gate_full, grad_up_full = grads
    hidden_out = hidden_all.reshape(TOKENS, TOPK, FF)
    grad_tokens = grad_all.astype(jnp.bfloat16)
    return hidden_out, grad_tokens, to_layout(grad_gate_full), to_layout(grad_up_full)
```

```python
import functools

import jax
import jax.numpy as jnp
from jax import lax
from jax.experimental import pallas as pl
from jax.experimental.pallas import tpu as pltpu
from jax.sharding import Mesh
from jax.sharding import PartitionSpec as P

D = 2048
FF = 768
TOPK = 4
SUB = 4
BLK = 192
TOK = 32
PAIRS = TOK * TOPK
NZ = 16
NQ = 32
CAP = 2
ROWS = NQ * NZ * CAP
NTOK = NZ * TOK
AXES = ("x", "yh", "core", "yl", "z")
PLANE = ("x", "yh", "core", "yl")
F32 = jnp.float32
BF16 = jnp.bfloat16
VMEM_LIMIT = 56 * 1024 * 1024
STEPS = (0, -4, 4, 8)


def dot(a, b):
    return lax.dot_general(a, b, (((1,), (0,)), ((), ())), preferred_element_type=F32)


def dot_last(a, b):
    return lax.dot_general(a, b, (((1,), (1,)), ((), ())), preferred_element_type=F32)


def dot_first(a, b):
    return lax.dot_general(a, b, (((0,), (0,)), ((), ())), preferred_element_type=F32)


def ones_where(mask):
    return jnp.where(mask, 1.0, 0.0).astype(BF16)


def iota(shape, dim):
    return lax.broadcasted_iota(jnp.int32, shape, dim)


def shift(block, offset):
    return lax.ppermute(block, "z", [(i, (i + offset) % NZ) for i in range(NZ)])


def turn(block, offset):
    return lax.ppermute(
        block, "z", [(i, i // SUB * SUB + (i + offset) % SUB) for i in range(NZ)]
    )


def params():
    return pltpu.CompilerParams(vmem_limit_bytes=VMEM_LIMIT)


def vmem():
    return pl.BlockSpec(memory_space=pltpu.VMEM)


def smem():
    return pl.BlockSpec(memory_space=pltpu.SMEM)


def pack_kernel(place, row_of, rank_of, gh, out):
    s = place[1]
    pairs = gh[...]
    rows = iota((PAIRS, PAIRS), 0)
    hit = rows == row_of[...]
    placed = [
        dot(ones_where(hit & (rank_of[...] == r)), pairs).astype(BF16) for r in range(CAP)
    ]
    source = iota((FF, CAP * BLK), 0)
    target = iota((FF, CAP * BLK), 1)
    for step in range(SUB):
        base = ((s + step) & 3) * BLK
        total = None
        for r in range(CAP):
            unit = target - r * BLK
            pick = ones_where((unit >= 0) & (unit < BLK) & (source == unit + base))
            part = dot(placed[r], pick)
            total = part if total is None else total + part
        out[:, step * CAP * BLK : (step + 1) * CAP * BLK] = total.astype(BF16)


def unpack_kernel(place, row_of, rank_of, slots, out):
    s = place[1]
    rows = iota((PAIRS, PAIRS), 1)
    hit = rows == row_of[...]
    source = iota((CAP * BLK, FF), 0)
    target = iota((CAP * BLK, FF), 1)
    total = jnp.zeros((PAIRS, FF), F32)
    for r in range(CAP):
        spread = jnp.zeros((PAIRS, FF), F32)
        unit = source - r * BLK
        for step in range(SUB):
            base = ((s + step) & 3) * BLK
            pick = ones_where((unit >= 0) & (unit < BLK) & (target == unit + base))
            spread += dot(slots[:, step * CAP * BLK : (step + 1) * CAP * BLK], pick)
        total += dot(ones_where(hit & (rank_of[...] == r)), spread.astype(BF16))
    out[...] = total.astype(BF16)


def slot_of(codes, place_z, quarter):
    expert = codes >> 1
    slot = (expert >> 2) * (NZ * CAP) + place_z * CAP + (codes & 1)
    return jnp.where((expert & 3) == quarter, slot, -1)


def select_kernel(place, tokens, out):
    tile = out.shape[0]
    first = pl.program_id(0) * tile
    codes = jnp.transpose(tokens[:, D:].astype(F32)).astype(jnp.int32)
    origin = codes[TOPK : TOPK + 1, :]
    slots = iota((tile, NTOK), 0) + first
    hit = None
    for k in range(TOPK):
        same = slots == slot_of(codes[k : k + 1, :], origin, place[0])
        hit = same if hit is None else hit | same
    out[...] = dot(ones_where(hit), tokens[:, :D]).astype(BF16)


def combine_kernel(place, codes, slots, out):
    tile = out.shape[0]
    marks = codes[...].astype(F32).astype(jnp.int32)
    origin = marks[:, TOPK : TOPK + 1]
    index = iota((tile, ROWS), 1)
    hit = None
    for k in range(TOPK):
        same = index == slot_of(marks[:, k : k + 1], origin, place[0])
        hit = same if hit is None else hit | same
    out[...] = dot(ones_where(hit), slots[...]).astype(BF16)


def row_of_block(m, place):
    source = m & (NQ - 1)
    quarter = (place[0] - ((m >> 5) & 3)) & 3
    member = (place[1] - (m >> 7)) & 3
    return source * (NZ * CAP) + (quarter * SUB + member) * CAP


def expert_kernel(place, x, dh_in, w_gate, w_up, h_out, d_gate_out, d_up_out, dx, h_sum):
    step = pl.program_id(0)
    tile = x.shape[0]
    first = step * tile
    rows = x[...]
    spread_at = iota((BLK, CAP * BLK), 1) - iota((BLK, CAP * BLK), 0)
    pick_at = iota((CAP * BLK, BLK), 0) - iota((CAP * BLK, BLK), 1)
    upstream = jnp.zeros((tile, BLK), F32)
    home = row_of_block(iota((tile, NTOK), 1), place)
    here = iota((tile, NTOK), 0) + first
    for r in range(CAP):
        part = dot(dh_in[...], ones_where(pick_at == r * BLK)).astype(BF16)
        upstream += dot(ones_where(here == home + r), part)
    gate = dot_last(rows, w_gate[...])
    up = dot_last(rows, w_up[...])
    sigmoid = jax.nn.sigmoid(gate)
    active = gate * sigmoid
    hidden = (active * up).astype(BF16)
    d_gate = (upstream * up * sigmoid * (1.0 + gate * (1.0 - sigmoid))).astype(BF16)
    d_up = (upstream * active).astype(BF16)
    d_gate_out[...] = d_gate
    d_up_out[...] = d_up
    dx[...] = (dot(d_gate, w_gate[...]) + dot(d_up, w_up[...])).astype(BF16)

    back_home = row_of_block(iota((NTOK, tile), 0), place)
    back_here = iota((NTOK, tile), 1) + first
    total = None
    for r in range(CAP):
        wide = dot(hidden, ones_where(spread_at == r * BLK)).astype(BF16)
        part = dot(ones_where(back_here == back_home + r), wide)
        total = part if total is None else total + part

    @pl.when(step == 0)
    def _():
        h_sum[...] = total

    @pl.when(step > 0)
    def _():
        h_sum[...] += total

    @pl.when(step == pl.num_programs(0) - 1)
    def _():
        h_out[...] = h_sum[...].astype(BF16)


def weights_kernel(x, d_gate, d_up, grad_gate, grad_up):
    grad_gate[...] = dot_first(d_gate[...], x[...]).astype(BF16)
    grad_up[...] = dot_first(d_up[...], x[...]).astype(BF16)


def on_device(tokens, expert_ids, grad_hidden, gate_blocks, up_blocks):
    z = lax.axis_index("z")
    quarter, member = z // SUB, z % SUB
    place = jnp.stack([quarter, member]).astype(jnp.int32)

    same = expert_ids[:, :, None, None] == expert_ids[None, None, :, :]
    before = (
        jnp.arange(TOK, dtype=jnp.int32)[:, None, None, None]
        > jnp.arange(TOK, dtype=jnp.int32)[None, None, :, None]
    )
    rank = jnp.sum((same & before).astype(jnp.int32), axis=(2, 3))
    codes = jnp.concatenate(
        [expert_ids * 2 + rank, jnp.full((TOK, 1), z, jnp.int32), jnp.zeros((TOK, 123), jnp.int32)],
        axis=1,
    ).astype(BF16)
    block = jnp.concatenate([tokens, codes], axis=1)

    near = jnp.stack([block, shift(block, 4), shift(block, -4), shift(block, 8)])
    column = jnp.concatenate(
        [
            near,
            shift(near, 1),
            shift(near, -1),
            shift(near[0:2], 2),
            shift(jnp.concatenate([near[0:1], near[2:3]]), -2),
        ]
    ).reshape(NTOK, D + 128)

    row_of = (expert_ids >> 2) * SUB + ((expert_ids - quarter) & 3)
    row_line, rank_line = row_of.reshape(1, PAIRS), rank.reshape(1, PAIRS)
    dh_send = pl.pallas_call(
        pack_kernel,
        out_shape=jax.ShapeDtypeStruct((PAIRS, SUB * CAP * BLK), BF16),
        in_specs=[smem(), vmem(), vmem(), vmem()],
        out_specs=vmem(),
        compiler_params=params(),
        name="pack",
    )(place, row_line, rank_line, grad_hidden.reshape(PAIRS, FF))
    dh_plane = lax.all_to_all(
        dh_send.reshape(NQ, SUB, SUB * CAP * BLK), PLANE, split_axis=0, concat_axis=0, tiled=True
    )
    dh_far = dh_plane.transpose(1, 0, 2)
    dh_quarter = jnp.stack([dh_far[0]] + [shift(dh_far[i], 4 * i) for i in range(1, SUB)])
    width = CAP * BLK
    dh_in = jnp.concatenate(
        [dh_quarter[:, :, :width]]
        + [turn(dh_quarter[:, :, i * width : (i + 1) * width], i) for i in range(1, SUB)]
    ).reshape(NTOK, width)

    tile = 256
    x_send = pl.pallas_call(
        select_kernel,
        out_shape=jax.ShapeDtypeStruct((ROWS, D), BF16),
        grid=(ROWS // tile,),
        in_specs=[smem(), pl.BlockSpec((NTOK, D + 128), lambda i: (0, 0))],
        out_specs=pl.BlockSpec((tile, D), lambda i: (i, 0)),
        compiler_params=params(),
        name="select",
    )(place, column)
    x_all = lax.all_to_all(
        x_send.reshape(NQ, NZ * CAP, D), PLANE, split_axis=0, concat_axis=0, tiled=True
    ).reshape(ROWS, D)

    w_gate, w_up = gate_blocks[0], up_blocks[0]
    whole = lambda i: (0, 0)
    h_all, d_gate, d_up, dx = pl.pallas_call(
        expert_kernel,
        out_shape=(
            jax.ShapeDtypeStruct((NTOK, width), BF16),
            jax.ShapeDtypeStruct((ROWS, BLK), BF16),
            jax.ShapeDtypeStruct((ROWS, BLK), BF16),
            jax.ShapeDtypeStruct((ROWS, D), BF16),
        ),
        grid=(ROWS // tile,),
        in_specs=[
            smem(),
            pl.BlockSpec((tile, D), lambda i: (i, 0)),
            pl.BlockSpec((NTOK, width), whole),
            pl.BlockSpec((BLK, D), whole),
            pl.BlockSpec((BLK, D), whole),
        ],
        out_specs=(
            pl.BlockSpec((NTOK, width), whole),
            pl.BlockSpec((tile, BLK), lambda i: (i, 0)),
            pl.BlockSpec((tile, BLK), lambda i: (i, 0)),
            pl.BlockSpec((tile, D), lambda i: (i, 0)),
        ),
        scratch_shapes=[pltpu.VMEM((NTOK, width), F32)],
        compiler_params=params(),
        name="expert",
    )(place, x_all, dh_in, w_gate, w_up)

    dx_back = lax.all_to_all(
        dx.reshape(NQ, NZ * CAP, D), PLANE, split_axis=0, concat_axis=0, tiled=True
    ).reshape(ROWS, D)

    h_turn = h_all.reshape(SUB, SUB, NQ, width)
    h_quarter = jnp.concatenate(
        [h_turn[0]] + [turn(h_turn[i], -i) for i in range(1, SUB)], axis=2
    )
    h_plane = jnp.stack([h_quarter[0]] + [shift(h_quarter[i], -4 * i) for i in range(1, SUB)])

    cols = D // 4
    grad_gate, grad_up = pl.pallas_call(
        weights_kernel,
        out_shape=(jax.ShapeDtypeStruct((BLK, D), BF16), jax.ShapeDtypeStruct((BLK, D), BF16)),
        grid=(4,),
        in_specs=[
            pl.BlockSpec((ROWS, cols), lambda i: (0, i)),
            pl.BlockSpec((ROWS, BLK), whole),
            pl.BlockSpec((ROWS, BLK), whole),
        ],
        out_specs=(pl.BlockSpec((BLK, cols), lambda i: (0, i)),) * 2,
        compiler_params=params(),
        cost_estimate=pl.CostEstimate(flops=4 * ROWS * BLK * D, bytes_accessed=6 << 20, transcendentals=0),
        name="weights",
    )(x_all, d_gate, d_up)

    part = pl.pallas_call(
        combine_kernel,
        out_shape=jax.ShapeDtypeStruct((NTOK, D), BF16),
        grid=(NTOK // 128,),
        in_specs=[
            smem(),
            pl.BlockSpec((128, 128), lambda i: (i, 0)),
            pl.BlockSpec((ROWS, D), whole),
        ],
        out_specs=pl.BlockSpec((128, D), lambda i: (i, 0)),
        compiler_params=params(),
        name="combine",
    )(place, column[:, D:], dx_back).reshape(NZ, TOK, D)

    from_up = shift(part[4:8], -1)
    from_down = shift(part[8:12], 1)
    far_up = shift(part[12:14], -2)
    far_down = shift(part[14:16], 2)
    held = [part[i].astype(F32) + from_up[i].astype(F32) + from_down[i].astype(F32) for i in range(4)]
    held[0] = held[0] + far_up[0].astype(F32) + far_down[0].astype(F32)
    held[1] = held[1] + far_up[1].astype(F32)
    held[2] = held[2] + far_down[1].astype(F32)
    grad_tokens = (
        held[0]
        + shift(held[1].astype(BF16), -4).astype(F32)
        + shift(held[2].astype(BF16), 4).astype(F32)
        + shift(held[3].astype(BF16), 8).astype(F32)
    ).astype(BF16)

    h_slots = lax.all_to_all(
        h_plane.transpose(1, 0, 2), PLANE, split_axis=0, concat_axis=0, tiled=True
    ).reshape(PAIRS, SUB * width)
    hidden = pl.pallas_call(
        unpack_kernel,
        out_shape=jax.ShapeDtypeStruct((PAIRS, FF), BF16),
        in_specs=[smem(), vmem(), vmem(), vmem()],
        out_specs=vmem(),
        compiler_params=params(),
        name="unpack",
    )(place, row_of.reshape(PAIRS, 1), rank.reshape(PAIRS, 1), h_slots)
    return hidden.reshape(TOK, TOPK, FF), grad_tokens, grad_gate[None], grad_up[None]


def solution(mesh):
    fine = Mesh(mesh.devices.reshape(4, 2, 2, 2, NZ), AXES)
    return jax.shard_map(
        on_device, mesh=fine, in_specs=(P(AXES),) * 5, out_specs=(P(AXES),) * 4, check_vma=False
    )
```

```python
import jax
import jax.numpy as jnp
from jax import lax
from jax.experimental import pallas as pl
from jax.experimental.pallas import tpu as pltpu
from jax.sharding import Mesh
from jax.sharding import PartitionSpec as P

D = 2048
FF = 768
TOPK = 4
SUB = 4
BLK = 192
PAIR = 2 * BLK
WIDE = D + PAIR
TOK = 32
PAIRS = TOK * TOPK
NZ = 16
NQ = 32
CAP = 2
HALF = NZ // 2
PER = HALF * CAP
ROWS = NQ * PER
NTOK = HALF * TOK
SENT = NQ * CAP
PLANE = ("x", "yh", "core", "yl")
EVEN = ("zq", "zm")
COLUMN = ("zq", "zm", "zl")
AXES = PLANE + COLUMN
F32 = jnp.float32
BF16 = jnp.bfloat16


def dot(a, b):
    return lax.dot_general(a, b, (((1,), (0,)), ((), ())), preferred_element_type=F32)


def dot_last(a, b):
    return lax.dot_general(a, b, (((1,), (1,)), ((), ())), preferred_element_type=F32)


def dot_first(a, b):
    return lax.dot_general(a, b, (((0,), (0,)), ((), ())), preferred_element_type=F32)


def ones_where(mask):
    return jnp.where(mask, 1.0, 0.0).astype(BF16)


def iota(shape, dim):
    return lax.broadcasted_iota(jnp.int32, shape, dim)


def shift(block, offset):
    return lax.ppermute(block, COLUMN, [(i, (i + offset) % NZ) for i in range(NZ)])


def swap(block):
    return lax.ppermute(block, COLUMN, [(i, i ^ 1) for i in range(NZ)])


def exchange(values, axes):
    return lax.all_to_all(values, axes, split_axis=0, concat_axis=0, tiled=True)


def params():
    return pltpu.CompilerParams(vmem_limit_bytes=56 * 1024 * 1024)


def vmem():
    return pl.BlockSpec(memory_space=pltpu.VMEM)


def smem():
    return pl.BlockSpec(memory_space=pltpu.SMEM)


def whole(i):
    return (0, 0)


def pack_kernel(row_of, gh, out):
    hit = iota((SUB * SENT, PAIRS), 0) == row_of[...]
    slots = dot(ones_where(hit), gh[...]).astype(BF16)
    for q in range(SUB):
        for m in range(2):
            out[q * 2 + m] = slots[q * SENT : (q + 1) * SENT, m * PAIR : (m + 1) * PAIR]


def unpack_kernel(row_of, received, out, slots):
    for q in range(SUB):
        for m in range(2):
            slots[q * SENT : (q + 1) * SENT, m * PAIR : (m + 1) * PAIR] = received[q * 2 + m]
    hit = iota((PAIRS, SUB * SENT), 1) == row_of[...]
    out[...] = dot(ones_where(hit), slots[...]).astype(BF16)


def slot_of(codes, origin, quarter):
    expert = codes >> 1
    slot = (expert >> 2) * PER + (origin >> 1) * CAP + (codes & 1)
    return jnp.where((expert & 3) == quarter, slot, -1)


def select_kernel(place, *refs):
    pieces, dh, out, codes_out, held = refs[:7], refs[7], refs[8], refs[9], refs[10]
    tile = out.shape[0]

    @pl.when(pl.program_id(0) == 0)
    def _():
        at = 0
        for piece in pieces:
            held[at : at + piece.shape[0]] = piece[...]
            at += piece.shape[0]
        codes_out[...] = held[:, D:]

    first = pl.program_id(0) * tile
    codes = jnp.transpose(held[:, D:].astype(F32)).astype(jnp.int32)
    origin = codes[TOPK : TOPK + 1, :]
    slots = iota((tile, NTOK), 0) + first
    hit = None
    for k in range(TOPK):
        same = slots == slot_of(codes[k : k + 1, :], origin, place[0])
        hit = same if hit is None else hit | same
    out[:, :D] = dot(ones_where(hit), held[:, :D]).astype(BF16)
    row = iota((tile, ROWS), 0) + first
    came = ((row >> 1) & (HALF - 1)) * SENT + (row >> 4) * CAP + (row & 1)
    out[:, D:] = dot(ones_where(iota((tile, ROWS), 1) == came), dh[...]).astype(BF16)


def combine_kernel(place, codes, slots, out, h_out):
    tile = out.shape[0]
    marks = codes[...].astype(F32).astype(jnp.int32)
    origin = marks[:, TOPK : TOPK + 1]
    index = iota((tile, ROWS), 1)
    hit = None
    for k in range(TOPK):
        same = index == slot_of(marks[:, k : k + 1], origin, place[0])
        hit = same if hit is None else hit | same
    out[...] = dot(ones_where(hit), slots[:, :D]).astype(BF16)
    tile = h_out.shape[0]
    sent = iota((tile, ROWS), 0) + pl.program_id(0) * tile
    row = ((sent >> 1) & (NQ - 1)) * PER + (sent >> 6) * CAP + (sent & 1)
    h_out[...] = dot(ones_where(iota((tile, ROWS), 1) == row), slots[:, D:]).astype(BF16)


def expert_kernel(
    place, x, gate_own, gate_other, up_own, up_other, back, d_gate_out, d_up_out, w_gate, w_up
):
    for parity in range(2):
        first, second = (gate_own, up_own), (gate_other, up_other)
        if parity:
            first, second = second, first

        @pl.when((pl.program_id(0) == 0) & (place[1] == parity))
        def _(first=first, second=second):
            w_gate[:BLK], w_up[:BLK] = first[0][...], first[1][...]
            w_gate[BLK:], w_up[BLK:] = second[0][...], second[1][...]

    rows = x[:, :D]
    upstream = x[:, D:].astype(F32)
    gate = dot_last(rows, w_gate[...])
    up = dot_last(rows, w_up[...])
    sigmoid = jax.nn.sigmoid(gate)
    active = gate * sigmoid
    back[:, D:] = (active * up).astype(BF16)
    d_gate = (upstream * up * sigmoid * (1.0 + gate * (1.0 - sigmoid))).astype(BF16)
    d_up = (upstream * active).astype(BF16)
    d_gate_out[...] = d_gate
    d_up_out[...] = d_up
    back[:, :D] = (dot(d_gate, w_gate[...]) + dot(d_up, w_up[...])).astype(BF16)


def weights_kernel(place, x, d_gate, d_up, own_gate, own_up, send_gate, send_up):
    even = place[1] == 0
    for d, own, send in ((d_gate, own_gate, send_gate), (d_up, own_up, send_up)):
        total = dot_first(d[...], x[...])
        own[...] = jnp.where(even, total[:BLK], total[BLK:])
        send[...] = jnp.where(even, total[BLK:], total[:BLK]).astype(BF16)


def on_device(tokens, expert_ids, grad_hidden, gate_blocks, up_blocks):
    z = lax.axis_index(COLUMN)
    place = jnp.stack([z // SUB, z % 2]).astype(jnp.int32)

    same = expert_ids[:, :, None, None] == expert_ids[None, None, :, :]
    before = (
        jnp.arange(TOK, dtype=jnp.int32)[:, None, None, None]
        > jnp.arange(TOK, dtype=jnp.int32)[None, None, :, None]
    )
    rank = jnp.sum((same & before).astype(jnp.int32), axis=(2, 3))
    codes = jnp.concatenate(
        [expert_ids * 2 + rank, jnp.full((TOK, 1), z, jnp.int32), jnp.zeros((TOK, 123), jnp.int32)],
        axis=1,
    ).astype(BF16)
    block = jnp.concatenate([tokens, codes], axis=1)

    half = TOK // 2
    below, above = shift(block, 4), shift(block, -4)

    row_of = (expert_ids & 3) * SENT + (expert_ids >> 2) * CAP + rank
    dh_send = pl.pallas_call(
        pack_kernel,
        out_shape=jax.ShapeDtypeStruct((HALF, SENT, PAIR), BF16),
        in_specs=[vmem(), vmem()],
        out_specs=vmem(),
        compiler_params=params(),
        name="pack",
    )(row_of.reshape(1, PAIRS), grad_hidden.reshape(PAIRS, FF))
    dh_send, below, above = lax.optimization_barrier((dh_send, below, above))
    dh = exchange(dh_send, EVEN).reshape(ROWS, PAIR)
    near_below = shift(jnp.concatenate([block, below]), 2)
    near_above = shift(jnp.concatenate([block, above]), -2)
    far_below, far_above = shift(below[:half], 4), shift(above[half:], -4)
    pieces = (block, below, above, far_below, far_above, near_below, near_above)

    tile = 256
    x_send, codes_all = pl.pallas_call(
        select_kernel,
        out_shape=(
            jax.ShapeDtypeStruct((ROWS, WIDE), BF16),
            jax.ShapeDtypeStruct((NTOK, 128), BF16),
        ),
        grid=(ROWS // tile,),
        in_specs=[smem()]
        + [pl.BlockSpec(piece.shape, whole) for piece in pieces]
        + [pl.BlockSpec((ROWS, PAIR), whole)],
        out_specs=(pl.BlockSpec((tile, WIDE), lambda i: (i, 0)), pl.BlockSpec((NTOK, 128), whole)),
        scratch_shapes=[pltpu.VMEM((NTOK, D + 128), BF16)],
        compiler_params=params(),
        name="select",
    )(place, *pieces, dh)

    gate_own, up_own = gate_blocks[0], up_blocks[0]
    x_send, gate_out, up_out = lax.optimization_barrier((x_send, gate_own, up_own))
    gate_other, up_other = swap(gate_out), swap(up_out)
    x_all = exchange(x_send.reshape(NQ, PER, WIDE), PLANE).reshape(ROWS, WIDE)

    by_rows = pl.BlockSpec((tile, WIDE), lambda i: (i, 0))
    by_rows_d = pl.BlockSpec((tile, PAIR), lambda i: (i, 0))
    back, d_gate, d_up = pl.pallas_call(
        expert_kernel,
        out_shape=(
            jax.ShapeDtypeStruct((ROWS, WIDE), BF16),
            jax.ShapeDtypeStruct((ROWS, PAIR), BF16),
            jax.ShapeDtypeStruct((ROWS, PAIR), BF16),
        ),
        grid=(ROWS // tile,),
        in_specs=[smem(), by_rows] + [pl.BlockSpec((BLK, D), whole)] * 4,
        out_specs=(by_rows, by_rows_d, by_rows_d),
        scratch_shapes=[pltpu.VMEM((PAIR, D), BF16)] * 2,
        compiler_params=params(),
        name="expert",
    )(place, x_all, gate_own, gate_other, up_own, up_other)

    returned = exchange(back.reshape(NQ, PER, WIDE), PLANE).reshape(ROWS, WIDE)

    cols = D // 4
    by_cols = pl.BlockSpec((BLK, cols), lambda i: (0, i))
    own_gate, own_up, send_gate, send_up = pl.pallas_call(
        weights_kernel,
        out_shape=(jax.ShapeDtypeStruct((BLK, D), F32),) * 2
        + (jax.ShapeDtypeStruct((BLK, D), BF16),) * 2,
        grid=(4,),
        in_specs=[
            smem(),
            pl.BlockSpec((ROWS, cols), lambda i: (0, i)),
            pl.BlockSpec((ROWS, PAIR), whole),
            pl.BlockSpec((ROWS, PAIR), whole),
        ],
        out_specs=(by_cols,) * 4,
        compiler_params=params(),
        cost_estimate=pl.CostEstimate(
            flops=4 * ROWS * PAIR * D, bytes_accessed=7 << 20, transcendentals=0
        ),
        name="weights",
    )(place, x_all, d_gate, d_up)
    recv_gate, recv_up = swap(send_gate), swap(send_up)

    part, h_send = pl.pallas_call(
        combine_kernel,
        out_shape=(
            jax.ShapeDtypeStruct((NTOK, D), BF16),
            jax.ShapeDtypeStruct((ROWS, PAIR), BF16),
        ),
        grid=(2,),
        in_specs=[
            smem(),
            pl.BlockSpec((NTOK // 2, 128), lambda i: (i, 0)),
            pl.BlockSpec((ROWS, WIDE), whole),
        ],
        out_specs=(
            pl.BlockSpec((NTOK // 2, D), lambda i: (i, 0)),
            pl.BlockSpec((ROWS // 2, PAIR), lambda i: (i, 0)),
        ),
        compiler_params=params(),
        name="combine",
    )(place, codes_all, returned)

    recv_gate, recv_up, part = lax.optimization_barrier((recv_gate, recv_up, part))
    grad_gate = (own_gate + recv_gate.astype(F32)).astype(BF16)
    grad_up = (own_up + recv_up.astype(F32)).astype(BF16)

    own, to_below, to_above = (part[i * TOK : (i + 1) * TOK].astype(F32) for i in range(3))
    at = 3 * TOK
    far_up = shift(part[at : at + half], -4).astype(F32)
    far_down = shift(part[at + half : at + TOK], 4).astype(F32)
    at += TOK
    near_up = shift(part[at : at + 2 * TOK], -2).astype(F32)
    near_down = shift(part[at + 2 * TOK :], 2).astype(F32)
    own = own + near_up[:TOK] + near_down[:TOK]
    to_below = to_below + near_up[TOK:]
    to_above = to_above + near_down[TOK:]
    to_below = jnp.concatenate([to_below[:half] + far_up, to_below[half:]])
    to_above = jnp.concatenate([to_above[:half], to_above[half:] + far_down])
    grad_tokens = (
        own
        + shift(to_below.astype(BF16), -4).astype(F32)
        + shift(to_above.astype(BF16), 4).astype(F32)
    ).astype(BF16)

    h_slots = exchange(h_send.reshape(HALF, SENT, PAIR), EVEN)
    hidden = pl.pallas_call(
        unpack_kernel,
        out_shape=jax.ShapeDtypeStruct((PAIRS, FF), BF16),
        in_specs=[vmem(), vmem()],
        out_specs=vmem(),
        scratch_shapes=[pltpu.VMEM((SUB * SENT, FF), BF16)],
        compiler_params=params(),
        name="unpack",
    )(row_of.reshape(PAIRS, 1), h_slots)
    return hidden.reshape(TOK, TOPK, FF), grad_tokens, grad_gate[None], grad_up[None]


def solution(mesh):
    fine = Mesh(mesh.devices.reshape(4, 2, 2, 2, SUB, 2, 2), AXES)
    return jax.shard_map(
        on_device, mesh=fine, in_specs=(P(AXES),) * 5, out_specs=(P(AXES),) * 4, check_vma=False
    )
```

```python
import jax
import jax.numpy as jnp
from jax import lax
from jax.experimental import pallas as pl
from jax.experimental.pallas import tpu as pltpu
from jax.sharding import Mesh
from jax.sharding import PartitionSpec as P

D = 2048
FF = 768
TOPK = 4
SUB = 4
BLK = 192
PAIR = 2 * BLK
WIDE = D + PAIR
TOK = 32
PAIRS = TOK * TOPK
NZ = 16
NQ = 32
CAP = 2
HALF = NZ // 2
PER = HALF * CAP
ROWS = NQ * PER
NTOK = HALF * TOK
SENT = NQ * CAP
PLANE = ("x", "yh", "core", "yl")
EVEN = ("zq", "zm")
COLUMN = ("zq", "zm", "zl")
AXES = PLANE + COLUMN
F32 = jnp.float32
BF16 = jnp.bfloat16


def dot(a, b):
    return lax.dot_general(a, b, (((1,), (0,)), ((), ())), preferred_element_type=F32)


def dot_last(a, b):
    return lax.dot_general(a, b, (((1,), (1,)), ((), ())), preferred_element_type=F32)


def dot_first(a, b):
    return lax.dot_general(a, b, (((0,), (0,)), ((), ())), preferred_element_type=F32)


def ones_where(mask):
    return jnp.where(mask, 1.0, 0.0).astype(BF16)


def iota(shape, dim):
    return lax.broadcasted_iota(jnp.int32, shape, dim)


def shift(block, offset):
    route = []
    for i in range(NZ):
        route += [(i, (i + offset) % NZ), (NZ + i, NZ + (i - offset) % NZ)]
    return lax.ppermute(block, ("core",) + COLUMN, route)


def swap(block):
    return lax.ppermute(block, COLUMN, [(i, i ^ 1) for i in range(NZ)])


def exchange(values, axes):
    return lax.all_to_all(values, axes, split_axis=0, concat_axis=0, tiled=True)


def params():
    return pltpu.CompilerParams(vmem_limit_bytes=56 * 1024 * 1024)


def vmem():
    return pl.BlockSpec(memory_space=pltpu.VMEM)


def smem():
    return pl.BlockSpec(memory_space=pltpu.SMEM)


def whole(i):
    return (0, 0)


def pack_kernel(row_of, gh, out):
    hit = iota((SUB * SENT, PAIRS), 0) == row_of[...]
    slots = dot(ones_where(hit), gh[...]).astype(BF16)
    for q in range(SUB):
        for m in range(2):
            out[q * 2 + m] = slots[q * SENT : (q + 1) * SENT, m * PAIR : (m + 1) * PAIR]


def unpack_kernel(row_of, received, out, slots):
    for q in range(SUB):
        for m in range(2):
            slots[q * SENT : (q + 1) * SENT, m * PAIR : (m + 1) * PAIR] = received[q * 2 + m]
    hit = iota((PAIRS, SUB * SENT), 1) == row_of[...]
    out[...] = dot(ones_where(hit), slots[...]).astype(BF16)


def slot_of(codes, origin, quarter):
    expert = codes >> 1
    slot = (expert >> 2) * PER + (origin >> 1) * CAP + (codes & 1)
    return jnp.where((expert & 3) == quarter, slot, -1)


def select_kernel(place, *refs):
    pieces, dh, out, codes_out, held = refs[:7], refs[7], refs[8], refs[9], refs[10]
    tile = out.shape[0]

    @pl.when(pl.program_id(0) == 0)
    def _():
        at = 0
        for piece in pieces:
            held[at : at + piece.shape[0]] = piece[...]
            at += piece.shape[0]
        codes_out[...] = held[:, D:]

    first = pl.program_id(0) * tile
    codes = jnp.transpose(held[:, D:].astype(F32)).astype(jnp.int32)
    origin = codes[TOPK : TOPK + 1, :]
    slots = iota((tile, NTOK), 0) + first
    hit = None
    for k in range(TOPK):
        same = slots == slot_of(codes[k : k + 1, :], origin, place[0])
        hit = same if hit is None else hit | same
    out[:, :D] = dot(ones_where(hit), held[:, :D]).astype(BF16)
    row = iota((tile, ROWS), 0) + first
    came = ((row >> 1) & (HALF - 1)) * SENT + (row >> 4) * CAP + (row & 1)
    out[:, D:] = dot(ones_where(iota((tile, ROWS), 1) == came), dh[...]).astype(BF16)


def combine_kernel(place, codes, slots, out, h_out):
    tile = out.shape[0]
    marks = codes[...].astype(F32).astype(jnp.int32)
    origin = marks[:, TOPK : TOPK + 1]
    index = iota((tile, ROWS), 1)
    hit = None
    for k in range(TOPK):
        same = index == slot_of(marks[:, k : k + 1], origin, place[0])
        hit = same if hit is None else hit | same
    out[...] = dot(ones_where(hit), slots[:, :D]).astype(BF16)
    tile = h_out.shape[0]
    sent = iota((tile, ROWS), 0) + pl.program_id(0) * tile
    row = ((sent >> 1) & (NQ - 1)) * PER + (sent >> 6) * CAP + (sent & 1)
    h_out[...] = dot(ones_where(iota((tile, ROWS), 1) == row), slots[:, D:]).astype(BF16)


def expert_kernel(
    place, x, gate_own, gate_other, up_own, up_other, back, d_gate_out, d_up_out, w_gate, w_up
):
    for parity in range(2):
        first, second = (gate_own, up_own), (gate_other, up_other)
        if parity:
            first, second = second, first

        @pl.when((pl.program_id(0) == 0) & (place[1] == parity))
        def _(first=first, second=second):
            w_gate[:BLK], w_up[:BLK] = first[0][...], first[1][...]
            w_gate[BLK:], w_up[BLK:] = second[0][...], second[1][...]

    rows = x[:, :D]
    upstream = x[:, D:].astype(F32)
    gate = dot_last(rows, w_gate[...])
    up = dot_last(rows, w_up[...])
    sigmoid = jax.nn.sigmoid(gate)
    active = gate * sigmoid
    back[:, D:] = (active * up).astype(BF16)
    d_gate = (upstream * up * sigmoid * (1.0 + gate * (1.0 - sigmoid))).astype(BF16)
    d_up = (upstream * active).astype(BF16)
    d_gate_out[...] = d_gate
    d_up_out[...] = d_up
    back[:, :D] = (dot(d_gate, w_gate[...]) + dot(d_up, w_up[...])).astype(BF16)


def weights_kernel(place, x, d_gate, d_up, own_gate, own_up, send_gate, send_up):
    even = place[1] == 0
    for d, own, send in ((d_gate, own_gate, send_gate), (d_up, own_up, send_up)):
        total = dot_first(d[...], x[...])
        own[...] = jnp.where(even, total[:BLK], total[BLK:])
        send[...] = jnp.where(even, total[BLK:], total[:BLK]).astype(BF16)


def on_device(tokens, expert_ids, grad_hidden, gate_blocks, up_blocks):
    z = lax.axis_index(COLUMN)
    place = jnp.stack([z // SUB, z % 2]).astype(jnp.int32)

    same = expert_ids[:, :, None, None] == expert_ids[None, None, :, :]
    before = (
        jnp.arange(TOK, dtype=jnp.int32)[:, None, None, None]
        > jnp.arange(TOK, dtype=jnp.int32)[None, None, :, None]
    )
    rank = jnp.sum((same & before).astype(jnp.int32), axis=(2, 3))
    codes = jnp.concatenate(
        [expert_ids * 2 + rank, jnp.full((TOK, 1), z, jnp.int32), jnp.zeros((TOK, 123), jnp.int32)],
        axis=1,
    ).astype(BF16)
    block = jnp.concatenate([tokens, codes], axis=1)

    half = TOK // 2
    below, above = shift(block, 4), shift(block, -4)

    row_of = (expert_ids & 3) * SENT + (expert_ids >> 2) * CAP + rank
    dh_send = pl.pallas_call(
        pack_kernel,
        out_shape=jax.ShapeDtypeStruct((HALF, SENT, PAIR), BF16),
        in_specs=[vmem(), vmem()],
        out_specs=vmem(),
        compiler_params=params(),
        name="pack",
    )(row_of.reshape(1, PAIRS), grad_hidden.reshape(PAIRS, FF))
    dh_send, below, above = lax.optimization_barrier((dh_send, below, above))
    dh = exchange(dh_send, EVEN).reshape(ROWS, PAIR)
    near_below = shift(jnp.concatenate([block, below]), 2)
    near_above = shift(jnp.concatenate([block, above]), -2)
    far_below, far_above = shift(below[:half], 4), shift(above[half:], -4)

    gate_own, up_own = gate_blocks[0], up_blocks[0]
    near_below, near_above, gate_out, up_out = lax.optimization_barrier(
        (near_below, near_above, gate_own, up_own)
    )
    gate_other, up_other = swap(gate_out), swap(up_out)
    pieces = (block, below, above, far_below, far_above, near_below, near_above)

    tile = 256
    x_send, codes_all = pl.pallas_call(
        select_kernel,
        out_shape=(
            jax.ShapeDtypeStruct((ROWS, WIDE), BF16),
            jax.ShapeDtypeStruct((NTOK, 128), BF16),
        ),
        grid=(ROWS // tile,),
        in_specs=[smem()]
        + [pl.BlockSpec(piece.shape, whole) for piece in pieces]
        + [pl.BlockSpec((ROWS, PAIR), whole)],
        out_specs=(pl.BlockSpec((tile, WIDE), lambda i: (i, 0)), pl.BlockSpec((NTOK, 128), whole)),
        scratch_shapes=[pltpu.VMEM((NTOK, D + 128), BF16)],
        compiler_params=params(),
        name="select",
    )(place, *pieces, dh)

    x_all = exchange(x_send.reshape(NQ, PER, WIDE), PLANE).reshape(ROWS, WIDE)

    by_rows = pl.BlockSpec((tile, WIDE), lambda i: (i, 0))
    by_rows_d = pl.BlockSpec((tile, PAIR), lambda i: (i, 0))
    back, d_gate, d_up = pl.pallas_call(
        expert_kernel,
        out_shape=(
            jax.ShapeDtypeStruct((ROWS, WIDE), BF16),
            jax.ShapeDtypeStruct((ROWS, PAIR), BF16),
            jax.ShapeDtypeStruct((ROWS, PAIR), BF16),
        ),
        grid=(ROWS // tile,),
        in_specs=[smem(), by_rows] + [pl.BlockSpec((BLK, D), whole)] * 4,
        out_specs=(by_rows, by_rows_d, by_rows_d),
        scratch_shapes=[pltpu.VMEM((PAIR, D), BF16)] * 2,
        compiler_params=params(),
        name="expert",
    )(place, x_all, gate_own, gate_other, up_own, up_other)

    returned = exchange(back.reshape(NQ, PER, WIDE), PLANE).reshape(ROWS, WIDE)

    cols = D // 4
    by_cols = pl.BlockSpec((BLK, cols), lambda i: (0, i))
    own_gate, own_up, send_gate, send_up = pl.pallas_call(
        weights_kernel,
        out_shape=(jax.ShapeDtypeStruct((BLK, D), F32),) * 2
        + (jax.ShapeDtypeStruct((BLK, D), BF16),) * 2,
        grid=(4,),
        in_specs=[
            smem(),
            pl.BlockSpec((ROWS, cols), lambda i: (0, i)),
            pl.BlockSpec((ROWS, PAIR), whole),
            pl.BlockSpec((ROWS, PAIR), whole),
        ],
        out_specs=(by_cols,) * 4,
        compiler_params=params(),
        cost_estimate=pl.CostEstimate(
            flops=4 * ROWS * PAIR * D, bytes_accessed=7 << 20, transcendentals=0
        ),
        name="weights",
    )(place, x_all, d_gate, d_up)
    recv_gate, recv_up = swap(send_gate), swap(send_up)

    part, h_send = pl.pallas_call(
        combine_kernel,
        out_shape=(
            jax.ShapeDtypeStruct((NTOK, D), BF16),
            jax.ShapeDtypeStruct((ROWS, PAIR), BF16),
        ),
        grid=(2,),
        in_specs=[
            smem(),
            pl.BlockSpec((NTOK // 2, 128), lambda i: (i, 0)),
            pl.BlockSpec((ROWS, WIDE), whole),
        ],
        out_specs=(
            pl.BlockSpec((NTOK // 2, D), lambda i: (i, 0)),
            pl.BlockSpec((ROWS // 2, PAIR), lambda i: (i, 0)),
        ),
        compiler_params=params(),
        name="combine",
    )(place, codes_all, returned)

    recv_gate, recv_up, part = lax.optimization_barrier((recv_gate, recv_up, part))
    grad_gate = (own_gate + recv_gate.astype(F32)).astype(BF16)
    grad_up = (own_up + recv_up.astype(F32)).astype(BF16)

    own, to_below, to_above = (part[i * TOK : (i + 1) * TOK].astype(F32) for i in range(3))
    at = 3 * TOK
    far_up = shift(part[at : at + half], -4).astype(F32)
    far_down = shift(part[at + half : at + TOK], 4).astype(F32)
    at += TOK
    near_up, near_down = shift(part[at : at + 2 * TOK], -2), shift(part[at + 2 * TOK :], 2)
    near_up, near_down = near_up.astype(F32), near_down.astype(F32)
    own = own + near_up[:TOK] + near_down[:TOK]
    to_below = to_below + near_up[TOK:]
    to_above = to_above + near_down[TOK:]
    to_below = jnp.concatenate([to_below[:half] + far_up, to_below[half:]])
    to_above = jnp.concatenate([to_above[:half], to_above[half:] + far_down])
    h_slots = exchange(h_send.reshape(HALF, SENT, PAIR), EVEN)
    hidden = pl.pallas_call(
        unpack_kernel,
        out_shape=jax.ShapeDtypeStruct((PAIRS, FF), BF16),
        in_specs=[vmem(), vmem()],
        out_specs=vmem(),
        scratch_shapes=[pltpu.VMEM((SUB * SENT, FF), BF16)],
        compiler_params=params(),
        name="unpack",
    )(row_of.reshape(PAIRS, 1), h_slots)
    hidden = hidden.reshape(TOK, TOPK, FF)
    from_above, from_below = shift(to_below.astype(BF16), -4), shift(to_above.astype(BF16), 4)
    hidden, from_above, from_below = lax.optimization_barrier((hidden, from_above, from_below))
    grad_tokens = (own + from_above.astype(F32) + from_below.astype(F32)).astype(BF16)
    return hidden, grad_tokens, grad_gate[None], grad_up[None]


def solution(mesh):
    fine = Mesh(mesh.devices.reshape(4, 2, 2, 2, SUB, 2, 2), AXES)
    return jax.shard_map(
        on_device, mesh=fine, in_specs=(P(AXES),) * 5, out_specs=(P(AXES),) * 4, check_vma=False
    )
```

```python
import jax
import jax.numpy as jnp
from jax import lax
from jax.experimental import pallas as pl
from jax.experimental.pallas import tpu as pltpu
from jax.sharding import Mesh
from jax.sharding import PartitionSpec as P

D = 2048
FF = 768
TOPK = 4
SUB = 4
BLK = 192
PAIR = 2 * BLK
WIDE = D + PAIR
TOK = 32
PAIRS = TOK * TOPK
NZ = 16
NQ = 32
CAP = 2
HALF = NZ // 2
PER = HALF * CAP
ROWS = NQ * PER
NTOK = HALF * TOK
SENT = NQ * CAP
PLANE = ("x", "yh", "core", "yl")
EVEN = ("zq", "zm")
COLUMN = ("zq", "zm", "zl")
AXES = PLANE + COLUMN
F32 = jnp.float32
BF16 = jnp.bfloat16


def dot(a, b):
    return lax.dot_general(a, b, (((1,), (0,)), ((), ())), preferred_element_type=F32)


def dot_last(a, b):
    return lax.dot_general(a, b, (((1,), (1,)), ((), ())), preferred_element_type=F32)


def dot_first(a, b):
    return lax.dot_general(a, b, (((0,), (0,)), ((), ())), preferred_element_type=F32)


def ones_where(mask):
    return jnp.where(mask, 1.0, 0.0).astype(BF16)


def iota(shape, dim):
    return lax.broadcasted_iota(jnp.int32, shape, dim)


def shift(block, offset):
    route = []
    for i in range(NZ):
        route += [(i, (i + offset) % NZ), (NZ + i, NZ + (i - offset) % NZ)]
    return lax.ppermute(block, ("core",) + COLUMN, route)


def swap(block):
    return lax.ppermute(block, COLUMN, [(i, i ^ 1) for i in range(NZ)])


def exchange(values, axes):
    return lax.all_to_all(values, axes, split_axis=0, concat_axis=0, tiled=True)


def params():
    return pltpu.CompilerParams(vmem_limit_bytes=56 * 1024 * 1024)


def vmem():
    return pl.BlockSpec(memory_space=pltpu.VMEM)


def smem():
    return pl.BlockSpec(memory_space=pltpu.SMEM)


def whole(i):
    return (0, 0)


def pack_kernel(row_of, gh, out):
    hit = iota((SUB * SENT, PAIRS), 0) == row_of[...]
    slots = dot(ones_where(hit), gh[...]).astype(BF16)
    for q in range(SUB):
        for m in range(2):
            out[q * 2 + m] = slots[q * SENT : (q + 1) * SENT, m * PAIR : (m + 1) * PAIR]


def unpack_kernel(row_of, received, out, slots):
    for q in range(SUB):
        for m in range(2):
            slots[q * SENT : (q + 1) * SENT, m * PAIR : (m + 1) * PAIR] = received[q * 2 + m]
    hit = iota((PAIRS, SUB * SENT), 1) == row_of[...]
    out[...] = dot(ones_where(hit), slots[...]).astype(BF16)


def slot_of(codes, origin, quarter):
    expert = codes >> 1
    slot = (expert >> 2) * PER + (origin >> 1) * CAP + (codes & 1)
    return jnp.where((expert & 3) == quarter, slot, -1)


def select_kernel(place, *refs):
    pieces, dh, out, codes_out, held = refs[:6], refs[6], refs[7], refs[8], refs[9]
    tile = out.shape[0]

    @pl.when(pl.program_id(0) == 0)
    def _():
        at = 0
        for piece in pieces:
            held[at : at + piece.shape[0]] = piece[...]
            at += piece.shape[0]
        codes_out[...] = held[:, D:]

    first = pl.program_id(0) * tile
    codes = jnp.transpose(held[:, D:].astype(F32)).astype(jnp.int32)
    origin = codes[TOPK : TOPK + 1, :]
    slots = iota((tile, NTOK), 0) + first
    hit = None
    for k in range(TOPK):
        same = slots == slot_of(codes[k : k + 1, :], origin, place[0])
        hit = same if hit is None else hit | same
    out[:, :D] = dot(ones_where(hit), held[:, :D]).astype(BF16)
    row = iota((tile, ROWS), 0) + first
    came = ((row >> 1) & (HALF - 1)) * SENT + (row >> 4) * CAP + (row & 1)
    out[:, D:] = dot(ones_where(iota((tile, ROWS), 1) == came), dh[...]).astype(BF16)


def combine_kernel(place, codes, slots, out, h_out):
    tile = out.shape[0]
    marks = codes[...].astype(F32).astype(jnp.int32)
    origin = marks[:, TOPK : TOPK + 1]
    index = iota((tile, ROWS), 1)
    hit = None
    for k in range(TOPK):
        same = index == slot_of(marks[:, k : k + 1], origin, place[0])
        hit = same if hit is None else hit | same
    out[...] = dot(ones_where(hit), slots[:, :D]).astype(BF16)
    tile = h_out.shape[0]
    sent = iota((tile, ROWS), 0) + pl.program_id(0) * tile
    row = ((sent >> 1) & (NQ - 1)) * PER + (sent >> 6) * CAP + (sent & 1)
    h_out[...] = dot(ones_where(iota((tile, ROWS), 1) == row), slots[:, D:]).astype(BF16)


def expert_kernel(
    place, x, gate_own, gate_other, up_own, up_other, back, d_gate_out, d_up_out, w_gate, w_up
):
    for parity in range(2):
        first, second = (gate_own, up_own), (gate_other, up_other)
        if parity:
            first, second = second, first

        @pl.when((pl.program_id(0) == 0) & (place[1] == parity))
        def _(first=first, second=second):
            w_gate[:BLK], w_up[:BLK] = first[0][...], first[1][...]
            w_gate[BLK:], w_up[BLK:] = second[0][...], second[1][...]

    rows = x[:, :D]
    upstream = x[:, D:].astype(F32)
    gate = dot_last(rows, w_gate[...])
    up = dot_last(rows, w_up[...])
    sigmoid = jax.nn.sigmoid(gate)
    active = gate * sigmoid
    back[:, D:] = (active * up).astype(BF16)
    d_gate = (upstream * up * sigmoid * (1.0 + gate * (1.0 - sigmoid))).astype(BF16)
    d_up = (upstream * active).astype(BF16)
    d_gate_out[...] = d_gate
    d_up_out[...] = d_up
    back[:, :D] = (dot(d_gate, w_gate[...]) + dot(d_up, w_up[...])).astype(BF16)


def weights_kernel(place, x, d_gate, d_up, own_gate, own_up, send_gate, send_up):
    even = place[1] == 0
    for d, own, send in ((d_gate, own_gate, send_gate), (d_up, own_up, send_up)):
        total = dot_first(d[...], x[...])
        own[...] = jnp.where(even, total[:BLK], total[BLK:])
        send[...] = jnp.where(even, total[BLK:], total[:BLK]).astype(BF16)


def on_device(tokens, expert_ids, grad_hidden, gate_blocks, up_blocks):
    z = lax.axis_index(COLUMN)
    place = jnp.stack([z // SUB, z % 2]).astype(jnp.int32)

    same = expert_ids[:, :, None, None] == expert_ids[None, None, :, :]
    before = (
        jnp.arange(TOK, dtype=jnp.int32)[:, None, None, None]
        > jnp.arange(TOK, dtype=jnp.int32)[None, None, :, None]
    )
    rank = jnp.sum((same & before).astype(jnp.int32), axis=(2, 3))
    codes = jnp.concatenate(
        [expert_ids * 2 + rank, jnp.full((TOK, 1), z, jnp.int32), jnp.zeros((TOK, 123), jnp.int32)],
        axis=1,
    ).astype(BF16)
    block = jnp.concatenate([tokens, codes], axis=1)

    below, above = shift(block, 4), shift(block, -4)

    row_of = (expert_ids & 3) * SENT + (expert_ids >> 2) * CAP + rank
    dh_send = pl.pallas_call(
        pack_kernel,
        out_shape=jax.ShapeDtypeStruct((HALF, SENT, PAIR), BF16),
        in_specs=[vmem(), vmem()],
        out_specs=vmem(),
        compiler_params=params(),
        name="pack",
    )(row_of.reshape(1, PAIRS), grad_hidden.reshape(PAIRS, FF))
    dh_send, below, above = lax.optimization_barrier((dh_send, below, above))
    dh = exchange(dh_send, EVEN).reshape(ROWS, PAIR)
    near_below = shift(jnp.concatenate([block, below]), 2)
    near_above = shift(jnp.concatenate([block, above]), -2)
    far = shift(above, -4)

    gate_own, up_own = gate_blocks[0], up_blocks[0]
    near_below, near_above, gate_out, up_out = lax.optimization_barrier(
        (near_below, near_above, gate_own, up_own)
    )
    gate_other, up_other = swap(gate_out), swap(up_out)
    pieces = (block, below, above, far, near_below, near_above)

    tile = 256
    x_send, codes_all = pl.pallas_call(
        select_kernel,
        out_shape=(
            jax.ShapeDtypeStruct((ROWS, WIDE), BF16),
            jax.ShapeDtypeStruct((NTOK, 128), BF16),
        ),
        grid=(ROWS // tile,),
        in_specs=[smem()]
        + [pl.BlockSpec(piece.shape, whole) for piece in pieces]
        + [pl.BlockSpec((ROWS, PAIR), whole)],
        out_specs=(pl.BlockSpec((tile, WIDE), lambda i: (i, 0)), pl.BlockSpec((NTOK, 128), whole)),
        scratch_shapes=[pltpu.VMEM((NTOK, D + 128), BF16)],
        compiler_params=params(),
        name="select",
    )(place, *pieces, dh)

    x_all = exchange(x_send.reshape(NQ, PER, WIDE), PLANE).reshape(ROWS, WIDE)

    by_rows = pl.BlockSpec((tile, WIDE), lambda i: (i, 0))
    by_rows_d = pl.BlockSpec((tile, PAIR), lambda i: (i, 0))
    back, d_gate, d_up = pl.pallas_call(
        expert_kernel,
        out_shape=(
            jax.ShapeDtypeStruct((ROWS, WIDE), BF16),
            jax.ShapeDtypeStruct((ROWS, PAIR), BF16),
            jax.ShapeDtypeStruct((ROWS, PAIR), BF16),
        ),
        grid=(ROWS // tile,),
        in_specs=[smem(), by_rows] + [pl.BlockSpec((BLK, D), whole)] * 4,
        out_specs=(by_rows, by_rows_d, by_rows_d),
        scratch_shapes=[pltpu.VMEM((PAIR, D), BF16)] * 2,
        compiler_params=params(),
        name="expert",
    )(place, x_all, gate_own, gate_other, up_own, up_other)

    returned = exchange(back.reshape(NQ, PER, WIDE), PLANE).reshape(ROWS, WIDE)

    cols = D // 4
    by_cols = pl.BlockSpec((BLK, cols), lambda i: (0, i))
    own_gate, own_up, send_gate, send_up = pl.pallas_call(
        weights_kernel,
        out_shape=(jax.ShapeDtypeStruct((BLK, D), F32),) * 2
        + (jax.ShapeDtypeStruct((BLK, D), BF16),) * 2,
        grid=(4,),
        in_specs=[
            smem(),
            pl.BlockSpec((ROWS, cols), lambda i: (0, i)),
            pl.BlockSpec((ROWS, PAIR), whole),
            pl.BlockSpec((ROWS, PAIR), whole),
        ],
        out_specs=(by_cols,) * 4,
        compiler_params=params(),
        cost_estimate=pl.CostEstimate(
            flops=4 * ROWS * PAIR * D, bytes_accessed=7 << 20, transcendentals=0
        ),
        name="weights",
    )(place, x_all, d_gate, d_up)
    recv_gate, recv_up = swap(send_gate), swap(send_up)

    part, h_send = pl.pallas_call(
        combine_kernel,
        out_shape=(
            jax.ShapeDtypeStruct((NTOK, D), BF16),
            jax.ShapeDtypeStruct((ROWS, PAIR), BF16),
        ),
        grid=(2,),
        in_specs=[
            smem(),
            pl.BlockSpec((NTOK // 2, 128), lambda i: (i, 0)),
            pl.BlockSpec((ROWS, WIDE), whole),
        ],
        out_specs=(
            pl.BlockSpec((NTOK // 2, D), lambda i: (i, 0)),
            pl.BlockSpec((ROWS // 2, PAIR), lambda i: (i, 0)),
        ),
        compiler_params=params(),
        name="combine",
    )(place, codes_all, returned)

    recv_gate, recv_up, part = lax.optimization_barrier((recv_gate, recv_up, part))
    grad_gate = (own_gate + recv_gate.astype(F32)).astype(BF16)
    grad_up = (own_up + recv_up.astype(F32)).astype(BF16)

    own, to_below, to_above = (part[i * TOK : (i + 1) * TOK].astype(F32) for i in range(3))
    at = 3 * TOK
    far_down = shift(part[at : at + TOK], 4).astype(F32)
    at += TOK
    near_up, near_down = shift(part[at : at + 2 * TOK], -2), shift(part[at + 2 * TOK :], 2)
    near_up, near_down = near_up.astype(F32), near_down.astype(F32)
    own = own + near_up[:TOK] + near_down[:TOK]
    to_below = to_below + near_up[TOK:]
    to_above = to_above + near_down[TOK:] + far_down
    h_slots = exchange(h_send.reshape(HALF, SENT, PAIR), EVEN)
    hidden = pl.pallas_call(
        unpack_kernel,
        out_shape=jax.ShapeDtypeStruct((PAIRS, FF), BF16),
        in_specs=[vmem(), vmem()],
        out_specs=vmem(),
        scratch_shapes=[pltpu.VMEM((SUB * SENT, FF), BF16)],
        compiler_params=params(),
        name="unpack",
    )(row_of.reshape(PAIRS, 1), h_slots)
    hidden = hidden.reshape(TOK, TOPK, FF)
    from_above, from_below = shift(to_below.astype(BF16), -4), shift(to_above.astype(BF16), 4)
    hidden, from_above, from_below = lax.optimization_barrier((hidden, from_above, from_below))
    grad_tokens = (own + from_above.astype(F32) + from_below.astype(F32)).astype(BF16)
    return hidden, grad_tokens, grad_gate[None], grad_up[None]


def solution(mesh):
    fine = Mesh(mesh.devices.reshape(4, 2, 2, 2, SUB, 2, 2), AXES)
    return jax.shard_map(
        on_device, mesh=fine, in_specs=(P(AXES),) * 5, out_specs=(P(AXES),) * 4, check_vma=False
    )
```

```python
import jax
import jax.numpy as jnp
from jax import lax
from jax.experimental import pallas as pl
from jax.experimental.pallas import tpu as pltpu
from jax.sharding import Mesh
from jax.sharding import PartitionSpec as P

D = 2048
FF = 768
TOPK = 4
SUB = 4
BLK = 192
PAIR = 2 * BLK
WIDE = D + PAIR
TOK = 32
PAIRS = TOK * TOPK
NZ = 16
NQ = 32
CAP = 2
HALF = NZ // 2
PER = HALF * CAP
ROWS = NQ * PER
NTOK = HALF * TOK
SENT = NQ * CAP
PLANE = ("x", "yh", "core", "yl")
EVEN = ("zq", "zm")
COLUMN = ("zq", "zm", "zl")
AXES = PLANE + COLUMN
F32 = jnp.float32
BF16 = jnp.bfloat16


def dot(a, b):
    return lax.dot_general(a, b, (((1,), (0,)), ((), ())), preferred_element_type=F32)


def dot_last(a, b):
    return lax.dot_general(a, b, (((1,), (1,)), ((), ())), preferred_element_type=F32)


def dot_first(a, b):
    return lax.dot_general(a, b, (((0,), (0,)), ((), ())), preferred_element_type=F32)


def ones_where(mask):
    return jnp.where(mask, 1.0, 0.0).astype(BF16)


def iota(shape, dim):
    return lax.broadcasted_iota(jnp.int32, shape, dim)


def shift(block, offset):
    route = []
    for i in range(NZ):
        route += [(i, (i + offset) % NZ), (NZ + i, NZ + (i - offset) % NZ)]
    return lax.ppermute(block, ("core",) + COLUMN, route)


def swap(block):
    return lax.ppermute(block, COLUMN, [(i, i ^ 1) for i in range(NZ)])


def exchange(values, axes):
    return lax.all_to_all(values, axes, split_axis=0, concat_axis=0, tiled=True)


def params():
    return pltpu.CompilerParams(vmem_limit_bytes=56 * 1024 * 1024)


def vmem():
    return pl.BlockSpec(memory_space=pltpu.VMEM)


def smem():
    return pl.BlockSpec(memory_space=pltpu.SMEM)


def whole(i):
    return (0, 0)


def pack_kernel(row_of, gh, out):
    hit = iota((SUB * SENT, PAIRS), 0) == row_of[...]
    slots = dot(ones_where(hit), gh[...]).astype(BF16)
    for q in range(SUB):
        for m in range(2):
            out[q * 2 + m] = slots[q * SENT : (q + 1) * SENT, m * PAIR : (m + 1) * PAIR]


def unpack_kernel(row_of, received, out, slots):
    for q in range(SUB):
        for m in range(2):
            slots[q * SENT : (q + 1) * SENT, m * PAIR : (m + 1) * PAIR] = received[q * 2 + m]
    hit = iota((PAIRS, SUB * SENT), 1) == row_of[...]
    out[...] = dot(ones_where(hit), slots[...]).astype(BF16)


def slot_of(codes, origin, quarter):
    expert = codes >> 1
    slot = (expert >> 2) * PER + (origin >> 1) * CAP + (codes & 1)
    return jnp.where((expert & 3) == quarter, slot, -1)


def select_kernel(place, *refs):
    pieces, dh, out, codes_out, held = refs[:6], refs[6], refs[7], refs[8], refs[9]
    tile = out.shape[0]

    @pl.when(pl.program_id(0) == 0)
    def _():
        at = 0
        for piece in pieces:
            held[at : at + piece.shape[0]] = piece[...]
            at += piece.shape[0]
        codes_out[...] = held[:, D:]

    first = pl.program_id(0) * tile
    codes = jnp.transpose(held[:, D:].astype(F32)).astype(jnp.int32)
    origin = codes[TOPK : TOPK + 1, :]
    slots = iota((tile, NTOK), 0) + first
    hit = None
    for k in range(TOPK):
        same = slots == slot_of(codes[k : k + 1, :], origin, place[0])
        hit = same if hit is None else hit | same
    out[:, :D] = dot(ones_where(hit), held[:, :D]).astype(BF16)
    row = iota((tile, ROWS), 0) + first
    came = ((row >> 1) & (HALF - 1)) * SENT + (row >> 4) * CAP + (row & 1)
    out[:, D:] = dot(ones_where(iota((tile, ROWS), 1) == came), dh[...]).astype(BF16)


def combine_kernel(place, codes, slots, out, h_out):
    tile = out.shape[0]
    marks = codes[...].astype(F32).astype(jnp.int32)
    origin = marks[:, TOPK : TOPK + 1]
    index = iota((tile, ROWS), 1)
    hit = None
    for k in range(TOPK):
        same = index == slot_of(marks[:, k : k + 1], origin, place[0])
        hit = same if hit is None else hit | same
    out[...] = dot(ones_where(hit), slots[:, :D]).astype(BF16)
    tile = h_out.shape[0]
    sent = iota((tile, ROWS), 0) + pl.program_id(0) * tile
    row = ((sent >> 1) & (NQ - 1)) * PER + (sent >> 6) * CAP + (sent & 1)
    h_out[...] = dot(ones_where(iota((tile, ROWS), 1) == row), slots[:, D:]).astype(BF16)


def expert_kernel(
    place, x, gate_own, gate_other, up_own, up_other, back, d_gate_out, d_up_out, w_gate, w_up
):
    for parity in range(2):
        first, second = (gate_own, up_own), (gate_other, up_other)
        if parity:
            first, second = second, first

        @pl.when((pl.program_id(0) == 0) & (place[1] == parity))
        def _(first=first, second=second):
            w_gate[:BLK], w_up[:BLK] = first[0][...], first[1][...]
            w_gate[BLK:], w_up[BLK:] = second[0][...], second[1][...]

    rows = x[:, :D]
    upstream = x[:, D:].astype(F32)
    gate = dot_last(rows, w_gate[...])
    up = dot_last(rows, w_up[...])
    sigmoid = jax.nn.sigmoid(gate)
    active = gate * sigmoid
    back[:, D:] = (active * up).astype(BF16)
    d_gate = (upstream * up * sigmoid * (1.0 + gate * (1.0 - sigmoid))).astype(BF16)
    d_up = (upstream * active).astype(BF16)
    d_gate_out[...] = d_gate
    d_up_out[...] = d_up
    back[:, :D] = (dot(d_gate, w_gate[...]) + dot(d_up, w_up[...])).astype(BF16)


def weights_kernel(place, x, d_gate, d_up, own_gate, own_up, send_gate, send_up):
    even = place[1] == 0
    for d, own, send in ((d_gate, own_gate, send_gate), (d_up, own_up, send_up)):
        total = dot_first(d[...], x[...])
        own[...] = jnp.where(even, total[:BLK], total[BLK:])
        send[...] = jnp.where(even, total[BLK:], total[:BLK]).astype(BF16)


def on_device(tokens, expert_ids, grad_hidden, gate_blocks, up_blocks):
    z = lax.axis_index(COLUMN)
    place = jnp.stack([z // SUB, z % 2]).astype(jnp.int32)

    same = expert_ids[:, :, None, None] == expert_ids[None, None, :, :]
    before = (
        jnp.arange(TOK, dtype=jnp.int32)[:, None, None, None]
        > jnp.arange(TOK, dtype=jnp.int32)[None, None, :, None]
    )
    rank = jnp.sum((same & before).astype(jnp.int32), axis=(2, 3))
    codes = jnp.concatenate(
        [expert_ids * 2 + rank, jnp.full((TOK, 1), z, jnp.int32), jnp.zeros((TOK, 123), jnp.int32)],
        axis=1,
    ).astype(BF16)
    block = jnp.concatenate([tokens, codes], axis=1)

    below, above = shift(block, 4), shift(block, -4)

    row_of = (expert_ids & 3) * SENT + (expert_ids >> 2) * CAP + rank
    dh_send = pl.pallas_call(
        pack_kernel,
        out_shape=jax.ShapeDtypeStruct((HALF, SENT, PAIR), BF16),
        in_specs=[vmem(), vmem()],
        out_specs=vmem(),
        compiler_params=params(),
        name="pack",
    )(row_of.reshape(1, PAIRS), grad_hidden.reshape(PAIRS, FF))
    dh_send, below, above = lax.optimization_barrier((dh_send, below, above))
    dh = exchange(dh_send, EVEN).reshape(ROWS, PAIR)
    near_below = shift(jnp.concatenate([block, below]), 2)
    near_above = shift(jnp.concatenate([block, above]), -2)
    far = shift(above, -4)

    gate_own, up_own = gate_blocks[0], up_blocks[0]
    near_below, near_above, w_out = lax.optimization_barrier(
        (near_below, near_above, jnp.concatenate([gate_own, up_own]))
    )
    w_other = swap(w_out)
    pieces = (block, below, above, far, near_below, near_above)

    tile = 256
    x_send, codes_all = pl.pallas_call(
        select_kernel,
        out_shape=(
            jax.ShapeDtypeStruct((ROWS, WIDE), BF16),
            jax.ShapeDtypeStruct((NTOK, 128), BF16),
        ),
        grid=(ROWS // tile,),
        in_specs=[smem()]
        + [pl.BlockSpec(piece.shape, whole) for piece in pieces]
        + [pl.BlockSpec((ROWS, PAIR), whole)],
        out_specs=(pl.BlockSpec((tile, WIDE), lambda i: (i, 0)), pl.BlockSpec((NTOK, 128), whole)),
        scratch_shapes=[pltpu.VMEM((NTOK, D + 128), BF16)],
        compiler_params=params(),
        name="select",
    )(place, *pieces, dh)

    x_all = exchange(x_send.reshape(NQ, PER, WIDE), PLANE).reshape(ROWS, WIDE)

    by_rows = pl.BlockSpec((tile, WIDE), lambda i: (i, 0))
    by_rows_d = pl.BlockSpec((tile, PAIR), lambda i: (i, 0))
    back, d_gate, d_up = pl.pallas_call(
        expert_kernel,
        out_shape=(
            jax.ShapeDtypeStruct((ROWS, WIDE), BF16),
            jax.ShapeDtypeStruct((ROWS, PAIR), BF16),
            jax.ShapeDtypeStruct((ROWS, PAIR), BF16),
        ),
        grid=(ROWS // tile,),
        in_specs=[smem(), by_rows] + [pl.BlockSpec((BLK, D), whole), pl.BlockSpec((BLK, D), whole)]
        + [pl.BlockSpec((BLK, D), whole), pl.BlockSpec((BLK, D), lambda i: (1, 0))],
        out_specs=(by_rows, by_rows_d, by_rows_d),
        scratch_shapes=[pltpu.VMEM((PAIR, D), BF16)] * 2,
        compiler_params=params(),
        name="expert",
    )(place, x_all, gate_own, w_other, up_own, w_other)

    returned = exchange(back.reshape(NQ, PER, WIDE), PLANE).reshape(ROWS, WIDE)

    cols = D // 4
    by_cols = pl.BlockSpec((BLK, cols), lambda i: (0, i))
    own_gate, own_up, send_gate, send_up = pl.pallas_call(
        weights_kernel,
        out_shape=(jax.ShapeDtypeStruct((BLK, D), F32),) * 2
        + (jax.ShapeDtypeStruct((BLK, D), BF16),) * 2,
        grid=(4,),
        in_specs=[
            smem(),
            pl.BlockSpec((ROWS, cols), lambda i: (0, i)),
            pl.BlockSpec((ROWS, PAIR), whole),
            pl.BlockSpec((ROWS, PAIR), whole),
        ],
        out_specs=(by_cols,) * 4,
        compiler_params=params(),
        cost_estimate=pl.CostEstimate(
            flops=4 * ROWS * PAIR * D, bytes_accessed=7 << 20, transcendentals=0
        ),
        name="weights",
    )(place, x_all, d_gate, d_up)
    recv_gate, recv_up = swap(send_gate), swap(send_up)

    part, h_send = pl.pallas_call(
        combine_kernel,
        out_shape=(
            jax.ShapeDtypeStruct((NTOK, D), BF16),
            jax.ShapeDtypeStruct((ROWS, PAIR), BF16),
        ),
        grid=(2,),
        in_specs=[
            smem(),
            pl.BlockSpec((NTOK // 2, 128), lambda i: (i, 0)),
            pl.BlockSpec((ROWS, WIDE), whole),
        ],
        out_specs=(
            pl.BlockSpec((NTOK // 2, D), lambda i: (i, 0)),
            pl.BlockSpec((ROWS // 2, PAIR), lambda i: (i, 0)),
        ),
        compiler_params=params(),
        name="combine",
    )(place, codes_all, returned)

    recv_gate, recv_up, part = lax.optimization_barrier((recv_gate, recv_up, part))
    grad_gate = (own_gate + recv_gate.astype(F32)).astype(BF16)
    grad_up = (own_up + recv_up.astype(F32)).astype(BF16)

    own, to_below, to_above = (part[i * TOK : (i + 1) * TOK].astype(F32) for i in range(3))
    at = 3 * TOK
    far_down = shift(part[at : at + TOK], 4).astype(F32)
    at += TOK
    near_up, near_down = shift(part[at : at + 2 * TOK], -2), shift(part[at + 2 * TOK :], 2)
    near_up, near_down = near_up.astype(F32), near_down.astype(F32)
    own = own + near_up[:TOK] + near_down[:TOK]
    to_below = to_below + near_up[TOK:]
    to_above = to_above + near_down[TOK:] + far_down
    h_slots = exchange(h_send.reshape(HALF, SENT, PAIR), EVEN)
    hidden = pl.pallas_call(
        unpack_kernel,
        out_shape=jax.ShapeDtypeStruct((PAIRS, FF), BF16),
        in_specs=[vmem(), vmem()],
        out_specs=vmem(),
        scratch_shapes=[pltpu.VMEM((SUB * SENT, FF), BF16)],
        compiler_params=params(),
        name="unpack",
    )(row_of.reshape(PAIRS, 1), h_slots)
    hidden = hidden.reshape(TOK, TOPK, FF)
    from_above, from_below = shift(to_below.astype(BF16), -4), shift(to_above.astype(BF16), 4)
    hidden, from_above, from_below = lax.optimization_barrier((hidden, from_above, from_below))
    grad_tokens = (own + from_above.astype(F32) + from_below.astype(F32)).astype(BF16)
    return hidden, grad_tokens, grad_gate[None], grad_up[None]


def solution(mesh):
    fine = Mesh(mesh.devices.reshape(4, 2, 2, 2, SUB, 2, 2), AXES)
    return jax.shard_map(
        on_device, mesh=fine, in_specs=(P(AXES),) * 5, out_specs=(P(AXES),) * 4, check_vma=False
    )
```
